256 devices in a mesh: gx: 16 (over z, core), gy: 16 (over y, x).
Axes of the slice: x: 4, y: 4, z: 8, core: 2. Of those that a mesh axis runs over, the one named last changes fastest.
Arguments:
- tensor: float32 [1024, 1024, 512], P('gx', 'gy'), may hold values from -6 to 6
- factor_two: float32 [1024, 128], P('gy', 'gx'), may hold values from -0.1875 to 0.1875
- factor_three: float32 [512, 128], P(('gx', 'gy')), may hold values from -0.25 to 0.25
Outputs:
- pair_three: float32 [1024, 1024, 128], P('gx', 'gy')
- pair_two: float32 [1024, 512, 128], P('gx', 'gy')
- mttkrp: float32 [1024, 128], P('gx')
The draws below stay inside these ranges and needn't reach their ends.
All inputs are finite; a program needn't handle non-finite values.
Results may differ from the reference program's by a relative error of at most 0.000084.
Values sent between devices are 32-bit elements; how exact they have to be, the bound alone decides.
A program may use at most 128 MiB of HBM per device.

```python
import jax
import jax.numpy as jnp
from jax import lax

K = 512
R = 128
I = 1024
J = 1024


def strengthened(entries, own_key, source, target, parts, factor):
    owner, partner = [(jnp.arange(entries.shape[position]) // (entries.shape[position] // parts)).reshape([-1 if axis == position else 1 for axis in range(entries.ndim)]) for position in (source, target)]
    chosen = jax.random.permutation(own_key, parts)[partner]
    strong = (owner == chosen) | (owner == (partner + parts // 2) % parts)
    return jnp.where(strong, factor * entries, entries)


def block_scale(rng, dims, split, low, high):
    loudness = 1.0
    for position, blocks in split:
        steps = jax.random.uniform(jax.random.fold_in(jax.random.fold_in(rng, 6), position), (blocks,), jnp.float32, low / len(split), high / len(split))
        loudness = loudness * jnp.repeat(jnp.exp(steps), dims[position] // blocks).reshape((-1,) + (1,) * (len(dims) - 1 - position))
    return loudness


def normal_values(rng, shape, scale, limit, pieces=(), held_as=jnp.bfloat16):
    loudness = block_scale(rng, shape, pieces, -0.22, 0.18) if pieces else 1.0
    drawn = jax.random.normal(rng, shape, jnp.float32) * scale * loudness
    return jnp.minimum(jnp.maximum(drawn, -limit), limit).astype(held_as)


def bell_draw_with(key, extent, scale, limit, shards, heavy, kind=jnp.bfloat16):
    array = scale * jax.random.normal(key, extent, jnp.float32)
    if shards:
        array = array * block_scale(key, extent, shards, -0.22, 0.18)
    return jnp.clip(strengthened(array, jax.random.fold_in(key, 3), *heavy), -limit, limit).astype(kind)


def setup_inputs(seed: int = 0) -> dict:
    streams_of = jax.random.split(jax.random.key(seed), 4)
    tensor = bell_draw_with(streams_of[0], (I, J, K), 1.0, 6.0, ((0, 16), (1, 16)), (1, 2, 16, 2.0), jnp.float32)
    factor_two = normal_values(streams_of[1], (J, R), J ** -0.5, 0.1875, ((0, 16), (1, 16)), jnp.float32)
    factor_three = normal_values(streams_of[2], (K, R), K ** -0.5, 0.25, ((0, 256),), jnp.float32)
    return {"tensor": tensor, "factor_two": factor_two, "factor_three": factor_three}


def reference(tensor, factor_two, factor_three):
    high = lax.Precision.HIGHEST
    pair_three = jnp.einsum('ijk,kr->ijr', tensor, factor_three, precision=high)
    pair_two = jnp.einsum('ijk,jr->ikr', tensor, factor_two, precision=high)
    mttkrp = jnp.einsum('ijr,jr->ir', pair_three, factor_two, precision=high)
    return pair_three, pair_two, mttkrp
```

```python
import functools

import jax
import jax.numpy as jnp
from jax import lax
from jax.experimental import pallas as pl
from jax.experimental.pallas import tpu as pltpu
from jax.sharding import PartitionSpec as P

MESH = pl.DeviceIdType.MESH
F32 = jnp.float32
BF16 = jnp.bfloat16
EAST, NORTH, WEST, SOUTH = range(4)

LEAVES = [
    ((EAST, EAST, NORTH, NORTH), NORTH),
    ((WEST, SOUTH), WEST),
    ((EAST, NORTH, NORTH), WEST),
    ((WEST, NORTH, NORTH), EAST),
    ((EAST, EAST, NORTH), SOUTH),
    ((WEST, NORTH), EAST),
    ((EAST, NORTH), SOUTH),
    ((EAST, SOUTH), NORTH),
    ((WEST,), EAST),
    ((SOUTH,), NORTH),
]
INNER = [
    ((EAST, EAST, SOUTH), (0, 1), (), NORTH),
    ((NORTH, NORTH), (2, 3), (), SOUTH),
    ((EAST, EAST), (4,), (0,), WEST),
    ((NORTH,), (5,), (1,), SOUTH),
    ((EAST,), (6, 7), (2,), WEST),
    ((), (8, 9), (4, 3), None),
]
STAGES = ((0, 1), (2, 3), (4,), (5,))
SKEW = 2
SUB = 4
ROWS = 8


def split(value):
    high = value.astype(BF16)
    return high, (value - high.astype(F32)).astype(BF16)


def kernel(
    tensor, two, three, pair_three, pair_two, mttkrp,
    whole, packed, raw, sent, got, out_three, out_two,
    tile_x, tile_y, tile_z, tile_c, col_z, col_c, near, two_own, weights, third, flip,
    local, sum_x, sum_y, total,
    load_sem, store_sem, raw_send, raw_recv, part_send, part_recv, gather_send, gather_recv,
):
    gx, gy = lax.axis_index("gx"), lax.axis_index("gy")
    z, c = gx // 2, lax.rem(gx, 2)
    y, x = gy // 4, lax.rem(gy, 4)
    groups = whole.shape[0] // ROWS

    def at_x(step):
        return (gx, y * 4 + lax.rem(x + step, 4))

    def at_y(step):
        return (gx, lax.rem(y + step, 4) * 4 + x)

    def at_z(step):
        return (lax.rem(z + step, 8) * 2 + c, gy)

    at_c = (z * 2 + 1 - c, gy)

    def east_of(d):
        return (1 - d) * lax.rem(d + 1, 2)

    def north_of(d):
        return (2 - d) * lax.rem(d, 2)

    def turned(d, turn):
        return lax.rem(d + turn, 4)

    def beside(d):
        return (gx, lax.rem(y + north_of(d) + 4, 4) * 4 + lax.rem(x + east_of(d) + 4, 4))

    def block_of(place, turn):
        tx, ty = x + 8, y + 8
        for d in place:
            tx, ty = tx - east_of(turned(d, turn)), ty - north_of(turned(d, turn))
        return lax.rem(ty, 4) * 4 + lax.rem(tx, 4)

    def load(g):
        rows = pl.ds(g * ROWS, ROWS)
        return pltpu.make_async_copy(tensor.at[rows], whole.at[rows], load_sem.at[g])

    for g in range(groups):
        load(g).start()

    barrier = pltpu.get_barrier_semaphore()
    peers = [at_x(s) for s in (1, 2, 3)] + [at_y(s) for s in (1, 2, 3)]
    peers += [at_z(s) for s in range(1, 8)] + [at_c]
    for peer in peers:
        pl.semaphore_signal(barrier, inc=1, device_id=peer, device_id_type=MESH)

    place = lax.broadcasted_iota(jnp.int32, (8, 128), 0)
    first, second = three[0:1, :], three[1:2, :]
    mine = jnp.where(place == 2 * x, first, jnp.where(place == 2 * x + 1, second, 0.0))
    tile_x[x] = mine
    flip[...] = jnp.zeros_like(flip)
    flip[0:64, 0:8] = two[...]
    col_z[z] = jnp.transpose(flip[...])[0:8, :]

    pl.semaphore_wait(barrier, len(peers))

    def gather(slot, ref, own, dst, device):
        return pltpu.make_async_remote_copy(
            src_ref=ref.at[own],
            dst_ref=ref.at[dst],
            send_sem=gather_send.at[slot],
            recv_sem=gather_recv.at[slot],
            device_id=device,
            device_id_type=MESH,
        )

    def ring(slot, ref, own, size, device):
        return [gather(slot + s - 1, ref, own, own, device(s)) for s in range(1, size)]

    first_copies = ring(0, tile_x, x, 4, at_x) + ring(3, col_z, z, 8, at_z)
    second_copies = ring(10, tile_y, y, 4, at_y) + [gather(13, col_c, c, c, at_c)]
    third_copies = ring(14, tile_z, z, 8, at_z)
    for d in range(4):
        third_copies.append(
            pltpu.make_async_remote_copy(
                src_ref=two_own,
                dst_ref=near.at[(d + 2) % 4],
                send_sem=gather_send.at[21 + d],
                recv_sem=gather_recv.at[21 + d],
                device_id=beside(d),
                device_id_type=MESH,
            )
        )
    fourth_copies = [gather(25, tile_c, c, c, at_c)]
    sum_one = [
        pltpu.make_async_remote_copy(
            src_ref=local.at[lax.rem(x + s, 4)],
            dst_ref=sum_x.at[x],
            send_sem=gather_send.at[25 + s],
            recv_sem=gather_recv.at[25 + s],
            device_id=at_x(s),
            device_id_type=MESH,
        )
        for s in (1, 2, 3)
    ]
    sum_two = ring(29, sum_y, y, 4, at_y)
    sum_three = ring(32, total, x, 4, at_x)

    def start(copies):
        for copy in copies:
            copy.start()

    def finish(copies):
        for copy in copies:
            copy.wait()

    start(first_copies)

    lane = lax.broadcasted_iota(jnp.int32, (64, 128), 1)
    low_half = lane < 64
    even = lax.rem(lane // 32, 2) == 0

    def pack(s):
        for quarter in range(4):
            a = [whole[s * SUB + i, :, pl.ds(quarter * 128, 128)] for i in range(SUB)]
            left = [jnp.where(low_half, a[i], pltpu.roll(a[i + 2], 64, 1)) for i in (0, 1)]
            right = [jnp.where(low_half, pltpu.roll(a[i], 64, 1), a[i + 2]) for i in (0, 1)]
            for half, (p, q) in enumerate((left, right)):
                packed[quarter * 4 + half * 2, s] = jnp.where(even, p, pltpu.roll(q, 32, 1))
                packed[quarter * 4 + half * 2 + 1, s] = jnp.where(even, pltpu.roll(p, 96, 1), q)

    def send_leaf(g, turn, n):
        place, d = LEAVES[n]
        return pltpu.make_async_remote_copy(
            src_ref=packed.at[block_of(place, turn), pl.ds(2 * g, 2)],
            dst_ref=raw.at[g, n],
            send_sem=raw_send.at[g],
            recv_sem=raw_recv.at[g],
            device_id=beside(turned(d, turn)),
            device_id_type=MESH,
        )

    @pl.loop(0, groups)
    def _(g):
        turn = lax.rem(g, 4)
        load(g).wait()
        pack(2 * g)
        pack(2 * g + 1)
        for n in range(len(LEAVES)):
            send_leaf(g, turn, n).start()

        @pl.when(g == 0)
        def _():
            finish(first_copies)
            tile_y[y] = tile_x[0] + tile_x[1] + tile_x[2] + tile_x[3]
            for k in range(8):
                col_c[c, pl.ds(8 * k, 8), :] = col_z[k]
            start(second_copies)

        @pl.when(g == 1)
        def _():
            finish(second_copies)
            for k in range(4):
                tile_z[z, pl.ds(8 * k, 8), :] = tile_y[k]
            for k in range(8):
                for core in range(2):
                    flip[pl.ds(16 * k + 8 * core, 8), :] = col_c[core, pl.ds(8 * k, 8), :]
            two_own[...] = jnp.transpose(flip[...])[0:64, :]
            start(third_copies)

        @pl.when(g == 3)
        def _():
            finish(third_copies)
            for k in range(8):
                tile_c[c, pl.ds(32 * k, 32), :] = tile_z[k]
            start(fourth_copies)

    finish(fourth_copies)
    for k in range(5):
        high, low = split(two_own[...] if k == 4 else near[k])
        weights[k, :, 0:128] = high
        weights[k, :, 128:256] = low
    for k in range(8):
        for core in range(2):
            high, low = split(tile_c[core, pl.ds(32 * k, 32), :])
            third[pl.ds(64 * k + 32 * core, 32), 0:128] = high
            third[pl.ds(64 * k + 32 * core, 32), 128:256] = low

    def times(value, weight, contract):
        dims = (((contract,), (0,)), ((), ()))
        out = sum(lax.dot_general(part, weight, dims, preferred_element_type=F32) for part in split(value))
        return out[:, 0:128] + out[:, 128:256]

    def store_three(g):
        rows = pl.ds(g * ROWS, ROWS)
        return pltpu.make_async_copy(out_three.at[rows], pair_three.at[rows], store_sem.at[0, g])

    def store_two(g):
        rows = pl.ds(g * ROWS, ROWS)
        return pltpu.make_async_copy(out_two.at[rows], pair_two.at[rows], store_sem.at[1, g])

    def contract_third(g):
        for i in range(0, ROWS, 2):
            rows = pl.ds(g * ROWS + i, 2)
            result = times(whole[rows].reshape(128, 512), third[...], 1).reshape(2, 64, 128)
            out_three[rows] = result
            sums = jnp.sum(result * two_own[...][None], axis=1)
            local[g // 2, pl.ds(lax.rem(g, 2) * 8 + i, 2), :] = sums
        store_three(g).start()

    def send_part(g, turn, n):
        return pltpu.make_async_remote_copy(
            src_ref=sent.at[g, n],
            dst_ref=got.at[g, n],
            send_sem=part_send.at[g, n],
            recv_sem=part_recv.at[g, n],
            device_id=beside(turned(INNER[n][3], turn)),
            device_id_type=MESH,
        )

    def inner(g, n):
        turn = lax.rem(g, 4)
        place, leaves, parts, d = INNER[n]
        own = block_of(place, turn)
        pieces, weight = [[packed[own, 2 * g + h] for h in (0, 1)]], [weights[4]]
        for leaf in leaves:
            pieces.append([raw[g, leaf, h] for h in (0, 1)])
            weight.append(weights[turned((LEAVES[leaf][1] + 2) % 4, turn)])
        stacked = jnp.concatenate([jnp.concatenate(piece, axis=1) for piece in pieces], axis=0)
        result = times(stacked, jnp.concatenate(weight, axis=0), 0)
        for part in parts:
            pltpu.make_async_copy(got.at[g, part], got.at[g, part], part_recv.at[g, part]).wait()
            result = result + got[g, part]
        if d is None:
            out_two[pl.ds(g * ROWS, ROWS)] = result.reshape(ROWS, 32, 128)
            store_two(g).start()
        else:
            sent[g, n] = result
            send_part(g, turn, n).start()

    @pl.loop(0, groups + 3 * SKEW)
    def _(step):
        @pl.when(step < groups)
        def _():
            pltpu.make_async_copy(raw.at[step], raw.at[step], raw_recv.at[step]).wait()

        for late, nodes in enumerate(STAGES):
            g = step - late * SKEW

            @pl.when((g >= 0) & (g < groups))
            def _(g=g, nodes=nodes):
                for n in nodes:
                    inner(g, n)

        @pl.when(step < groups)
        def _():
            contract_third(step)

        @pl.when(step == groups)
        def _():
            sum_x[x] = local[x]
            start(sum_one)

        @pl.when(step == groups + 2)
        def _():
            finish(sum_one)
            sum_y[y] = sum_x[0] + sum_x[1] + sum_x[2] + sum_x[3]
            start(sum_two)

        @pl.when(step == groups + 4)
        def _():
            finish(sum_two)
            total[x] = sum_y[0] + sum_y[1] + sum_y[2] + sum_y[3]
            start(sum_three)

    finish(sum_three)
    for k in range(4):
        mttkrp[pl.ds(16 * k, 16), :] = total[k]

    @pl.loop(0, groups)
    def _(g):
        store_three(g).wait()
        store_two(g).wait()
        pltpu.make_async_copy(raw.at[g], raw.at[g], raw_send.at[g]).wait()
        for n in range(5):
            pltpu.make_async_copy(sent.at[g, n], sent.at[g, n], part_send.at[g, n]).wait()


def per_device(tensor, two, three):
    rows = tensor.shape[0]
    groups, subs = rows // ROWS, rows // SUB
    hbm, vmem = pl.BlockSpec(memory_space=pl.ANY), pl.BlockSpec(memory_space=pltpu.VMEM)
    dma = pltpu.SemaphoreType.DMA
    return pl.pallas_call(
        kernel,
        name="pair_operators",
        out_shape=(
            jax.ShapeDtypeStruct((rows, 64, 128), F32),
            jax.ShapeDtypeStruct((rows, 32, 128), F32),
            jax.ShapeDtypeStruct((rows, 128), F32),
        ),
        in_specs=[hbm, vmem, vmem],
        out_specs=(hbm, hbm, vmem),
        scratch_shapes=[
            pltpu.VMEM(tensor.shape, F32),
            pltpu.VMEM((16, subs, 64, 128), F32),
            pltpu.VMEM((groups, len(LEAVES), 2, 64, 128), F32),
            pltpu.VMEM((groups, 5, 256, 128), F32),
            pltpu.VMEM((groups, 5, 256, 128), F32),
            pltpu.VMEM((rows, 64, 128), F32),
            pltpu.VMEM((rows, 32, 128), F32),
            pltpu.VMEM((4, 8, 128), F32),
            pltpu.VMEM((4, 8, 128), F32),
            pltpu.VMEM((8, 32, 128), F32),
            pltpu.VMEM((2, 256, 128), F32),
            pltpu.VMEM((8, 8, 128), F32),
            pltpu.VMEM((2, 64, 128), F32),
            pltpu.VMEM((4, 64, 128), F32),
            pltpu.VMEM((64, 128), F32),
            pltpu.VMEM((5, 64, 256), BF16),
            pltpu.VMEM((512, 256), BF16),
            pltpu.VMEM((128, 128), F32),
            pltpu.VMEM((4, 16, 128), F32),
            pltpu.VMEM((4, 16, 128), F32),
            pltpu.VMEM((4, 16, 128), F32),
            pltpu.VMEM((4, 16, 128), F32),
            dma((groups,)),
            dma((2, groups)),
            dma((groups,)),
            dma((groups,)),
            dma((groups, 5)),
            dma((groups, 5)),
            dma((35,)),
            dma((35,)),
        ],
        cost_estimate=pl.CostEstimate(flops=7 << 30, bytes_accessed=22 << 20, transcendentals=0),
        compiler_params=pltpu.CompilerParams(collective_id=0, has_side_effects=True, vmem_limit_bytes=56 << 20),
    )(tensor, two, three)


def solution(mesh):
    return jax.shard_map(
        per_device,
        mesh=mesh,
        in_specs=(P("gx", "gy", None), P("gy", "gx"), P(("gx", "gy"), None)),
        out_specs=(P("gx", "gy", None), P("gx", "gy", None), P("gx", None)),
        check_vma=False,
    )
```

```python
import functools

import jax
import jax.numpy as jnp
from jax import lax
from jax.experimental import pallas as pl
from jax.experimental.pallas import tpu as pltpu
from jax.sharding import PartitionSpec as P

MESH = pl.DeviceIdType.MESH
F32 = jnp.float32
BF16 = jnp.bfloat16
EAST, NORTH, WEST, SOUTH = range(4)

LEAVES = [
    ((EAST, EAST, NORTH, NORTH), NORTH),
    ((WEST, SOUTH), WEST),
    ((EAST, NORTH, NORTH), WEST),
    ((WEST, NORTH, NORTH), EAST),
    ((EAST, EAST, NORTH), SOUTH),
    ((WEST, NORTH), EAST),
    ((EAST, NORTH), SOUTH),
    ((EAST, SOUTH), NORTH),
    ((WEST,), EAST),
    ((SOUTH,), NORTH),
]
INNER = [
    ((EAST, EAST, SOUTH), (0, 1), (), NORTH),
    ((NORTH, NORTH), (2, 3), (), SOUTH),
    ((EAST, EAST), (4,), (0,), WEST),
    ((NORTH,), (5,), (1,), SOUTH),
    ((EAST,), (6, 7), (2,), WEST),
    ((), (8, 9), (4, 3), None),
]
STAGES = ((0, 1), (2, 3), (4,), (5,))
SKEW = 6
SUB = 4
ROWS = 8


def split(value):
    high = value.astype(BF16)
    return high, (value - high.astype(F32)).astype(BF16)


def kernel(
    tensor, two, three, pair_three, pair_two, mttkrp,
    whole, packed, raw, sent, got,
    tile_x, tile_y, tile_z, tile_c, col_z, col_c, near, two_own, weights, third, flip,
    local, sum_x, sum_y, total,
    load_sem, raw_send, raw_recv, part_send, part_recv, gather_send, gather_recv, ready_z, ready_c,
):
    gx, gy = lax.axis_index("gx"), lax.axis_index("gy")
    z, c = gx // 2, lax.rem(gx, 2)
    y, x = gy // 4, lax.rem(gy, 4)
    groups = whole.shape[0] // ROWS

    def at_x(step):
        return (gx, y * 4 + lax.rem(x + step, 4))

    def at_y(step):
        return (gx, lax.rem(y + step, 4) * 4 + x)

    def at_z(step):
        return (lax.rem(z + step, 8) * 2 + c, gy)

    at_c = (z * 2 + 1 - c, gy)

    def east_of(d):
        return (1 - d) * lax.rem(d + 1, 2)

    def north_of(d):
        return (2 - d) * lax.rem(d, 2)

    def turned(d, turn):
        return lax.rem(d + turn, 4)

    def beside(d):
        return (gx, lax.rem(y + north_of(d) + 4, 4) * 4 + lax.rem(x + east_of(d) + 4, 4))

    def block_of(place, turn):
        tx, ty = x + 8, y + 8
        for d in place:
            tx, ty = tx - east_of(turned(d, turn)), ty - north_of(turned(d, turn))
        return lax.rem(ty, 4) * 4 + lax.rem(tx, 4)

    def load(g):
        rows = pl.ds(g * ROWS, ROWS)
        return pltpu.make_async_copy(tensor.at[rows], whole.at[rows], load_sem.at[g])

    for g in range(groups):
        load(g).start()

    barrier = pltpu.get_barrier_semaphore()

    def greet(semaphore, device):
        pl.semaphore_signal(semaphore, inc=1, device_id=device, device_id_type=MESH)

    for s in (1, 2, 3):
        greet(barrier, at_x(s))
        greet(barrier, at_y(s))

    @pl.loop(z + 1, 8)
    def _(other):
        greet(barrier, (other * 2 + c, gy))

    @pl.when(c == 0)
    def _():
        greet(barrier, at_c)

    place = lax.broadcasted_iota(jnp.int32, (8, 128), 0)
    first, second = three[0:1, :], three[1:2, :]
    mine = jnp.where(place == 2 * x, first, jnp.where(place == 2 * x + 1, second, 0.0))
    tile_x[x] = mine
    flip[...] = jnp.zeros_like(flip)
    col_z[z] = jnp.zeros((8, 128), F32)
    col_z[z, :, 0:64] = two[...]

    pl.semaphore_wait(barrier, 6 + z + c)

    @pl.loop(0, z)
    def _(other):
        greet(ready_z, (other * 2 + c, gy))

    @pl.when(c == 1)
    def _():
        greet(ready_c, at_c)

    def gather(slot, ref, own, dst, device):
        return pltpu.make_async_remote_copy(
            src_ref=ref.at[own],
            dst_ref=ref.at[dst],
            send_sem=gather_send.at[slot],
            recv_sem=gather_recv.at[slot],
            device_id=device,
            device_id_type=MESH,
        )

    def ring(slot, ref, own, size, device):
        return [gather(slot + s - 1, ref, own, own, device(s)) for s in range(1, size)]

    three_x = ring(0, tile_x, x, 4, at_x)
    three_y = ring(3, tile_y, y, 4, at_y)
    three_z = ring(6, tile_z, z, 8, at_z)
    three_c = [gather(13, tile_c, c, c, at_c)]
    two_z = ring(14, col_z, z, 8, at_z)
    two_c = [gather(21, col_c, c, c, at_c)]
    two_near = [
        pltpu.make_async_remote_copy(
            src_ref=two_own,
            dst_ref=near.at[(d + 2) % 4],
            send_sem=gather_send.at[22 + d],
            recv_sem=gather_recv.at[22 + d],
            device_id=beside(d),
            device_id_type=MESH,
        )
        for d in range(4)
    ]
    sum_one = [
        pltpu.make_async_remote_copy(
            src_ref=local.at[lax.rem(x + s, 4)],
            dst_ref=sum_x.at[x],
            send_sem=gather_send.at[25 + s],
            recv_sem=gather_recv.at[25 + s],
            device_id=at_x(s),
            device_id_type=MESH,
        )
        for s in (1, 2, 3)
    ]
    sum_two = ring(29, sum_y, y, 4, at_y)
    sum_three = ring(32, total, x, 4, at_x)

    def start(copies):
        for copy in copies:
            copy.start()

    def finish(copies):
        for copy in copies:
            copy.wait()

    start(three_x)

    lane = lax.broadcasted_iota(jnp.int32, (64, 128), 1)
    low_half = lane < 64
    even = lax.rem(lane // 32, 2) == 0

    def pack(s):
        for quarter in range(4):
            a = [whole[s * SUB + i, :, pl.ds(quarter * 128, 128)] for i in range(SUB)]
            left = [jnp.where(low_half, a[i], pltpu.roll(a[i + 2], 64, 1)) for i in (0, 1)]
            right = [jnp.where(low_half, pltpu.roll(a[i], 64, 1), a[i + 2]) for i in (0, 1)]
            for half, (p, q) in enumerate((left, right)):
                packed[quarter * 4 + half * 2, s] = jnp.where(even, p, pltpu.roll(q, 32, 1))
                packed[quarter * 4 + half * 2 + 1, s] = jnp.where(even, pltpu.roll(p, 96, 1), q)

    def send_leaf(g, turn, n):
        place, d = LEAVES[n]
        return pltpu.make_async_remote_copy(
            src_ref=packed.at[block_of(place, turn), pl.ds(2 * g, 2)],
            dst_ref=raw.at[g, n],
            send_sem=raw_send.at[g],
            recv_sem=raw_recv.at[g],
            device_id=beside(turned(d, turn)),
            device_id_type=MESH,
        )

    @pl.loop(0, groups)
    def _(g):
        turn = lax.rem(g, 4)
        load(g).wait()
        pack(2 * g)
        pack(2 * g + 1)
        for n in range(len(LEAVES)):
            send_leaf(g, turn, n).start()

        @pl.when(g == 1)
        def _():
            finish(three_x)
            tile_y[y] = tile_x[0] + tile_x[1] + tile_x[2] + tile_x[3]
            start(three_y)

        @pl.when(g == 2)
        def _():
            @pl.when(z < 7)
            def _():
                pl.semaphore_wait(ready_z, 7 - z)

            start(two_z)

        @pl.when(g == 3)
        def _():
            finish(two_z)
            for k in range(8):
                col_c[c, pl.ds(8 * k, 8), :] = col_z[k]

            @pl.when(c == 0)
            def _():
                pl.semaphore_wait(ready_c, 1)

            start(two_c)
            finish(three_y)
            for k in range(4):
                tile_z[z, pl.ds(8 * k, 8), :] = tile_y[k]
            start(three_z)

        @pl.when(g == 4)
        def _():
            finish(two_c)
            for k in range(8):
                for core in range(2):
                    flip[pl.ds(16 * k + 8 * core, 8), :] = col_c[core, pl.ds(8 * k, 8), :]
            two_own[...] = jnp.transpose(flip[...])[0:64, :]
            start(two_near)
            finish(three_z)
            for k in range(8):
                tile_c[c, pl.ds(32 * k, 32), :] = tile_z[k]
            start(three_c)

    finish(three_c)
    finish(two_near)
    for k in range(5):
        high, low = split(two_own[...] if k == 4 else near[k])
        weights[k, :, 0:128] = high
        weights[k, :, 128:256] = low
    for k in range(8):
        for core in range(2):
            high, low = split(tile_c[core, pl.ds(32 * k, 32), :])
            third[pl.ds(64 * k + 32 * core, 32), 0:128] = high
            third[pl.ds(64 * k + 32 * core, 32), 128:256] = low

    def times(value, weight, contract):
        dims = (((contract,), (0,)), ((), ()))
        out = sum(lax.dot_general(part, weight, dims, preferred_element_type=F32) for part in split(value))
        return out[:, 0:128] + out[:, 128:256]

    def contract_third(g):
        for i in range(0, ROWS, 2):
            rows = pl.ds(g * ROWS + i, 2)
            result = times(whole[rows].reshape(128, 512), third[...], 1).reshape(2, 64, 128)
            pair_three[rows] = result
            sums = jnp.sum(result * two_own[...][None], axis=1)
            local[g // 2, pl.ds(lax.rem(g, 2) * 8 + i, 2), :] = sums

    def send_part(g, turn, n):
        return pltpu.make_async_remote_copy(
            src_ref=sent.at[g, n],
            dst_ref=got.at[g, n],
            send_sem=part_send.at[g, n],
            recv_sem=part_recv.at[g, n],
            device_id=beside(turned(INNER[n][3], turn)),
            device_id_type=MESH,
        )

    def inner(g, n):
        turn = lax.rem(g, 4)
        place, leaves, parts, d = INNER[n]
        own = block_of(place, turn)
        pieces, weight = [[packed[own, 2 * g + h] for h in (0, 1)]], [weights[4]]
        for leaf in leaves:
            pieces.append([raw[g, leaf, h] for h in (0, 1)])
            weight.append(weights[turned((LEAVES[leaf][1] + 2) % 4, turn)])
        stacked = jnp.concatenate([jnp.concatenate(piece, axis=1) for piece in pieces], axis=0)
        result = times(stacked, jnp.concatenate(weight, axis=0), 0)
        for part in parts:
            pltpu.make_async_copy(got.at[g, part], got.at[g, part], part_recv.at[g, part]).wait()
            result = result + got[g, part]
        if d is None:
            pair_two[pl.ds(g * ROWS, ROWS)] = result.reshape(ROWS, 32, 128)
        else:
            sent[g, n] = result
            send_part(g, turn, n).start()

    @pl.loop(0, groups + 3 * SKEW)
    def _(step):
        @pl.when(step < groups)
        def _():
            pltpu.make_async_copy(raw.at[step], raw.at[step], raw_recv.at[step]).wait()

        for late, nodes in enumerate(STAGES):
            g = step - late * SKEW

            @pl.when((g >= 0) & (g < groups))
            def _(g=g, nodes=nodes):
                for n in nodes:
                    inner(g, n)

        @pl.when(step < groups)
        def _():
            contract_third(step)

        @pl.when(step == groups)
        def _():
            sum_x[x] = local[x]
            start(sum_one)

        @pl.when(step == groups + 6)
        def _():
            finish(sum_one)
            sum_y[y] = sum_x[0] + sum_x[1] + sum_x[2] + sum_x[3]
            start(sum_two)

        @pl.when(step == groups + 12)
        def _():
            finish(sum_two)
            total[x] = sum_y[0] + sum_y[1] + sum_y[2] + sum_y[3]
            start(sum_three)

    finish(sum_three)
    for k in range(4):
        mttkrp[pl.ds(16 * k, 16), :] = total[k]

    @pl.loop(0, groups)
    def _(g):
        pltpu.make_async_copy(raw.at[g], raw.at[g], raw_send.at[g]).wait()
        for n in range(5):
            pltpu.make_async_copy(sent.at[g, n], sent.at[g, n], part_send.at[g, n]).wait()


def keep(*refs):
    sources, targets, sem = refs[:3], refs[3:6], refs[6]
    copies = []
    for source, target, parts in zip(sources, targets, (8, 4, 1)):
        size = source.shape[0] // parts
        for n in range(parts):
            rows = pl.ds(n * size, size)
            copies.append(pltpu.make_async_copy(source.at[rows], target.at[rows], sem.at[len(copies)]))
    for copy in copies:
        copy.start()
    for copy in copies:
        copy.wait()


def per_device(tensor, two, three):
    rows = tensor.shape[0]
    groups, subs = rows // ROWS, rows // SUB
    shapes = ((rows, 64, 128), (rows, 32, 128), (rows, 128))
    hbm, vmem = pl.BlockSpec(memory_space=pl.ANY), pl.BlockSpec(memory_space=pltpu.VMEM)
    dma, regular = pltpu.SemaphoreType.DMA, pltpu.SemaphoreType.REGULAR
    results = pl.pallas_call(
        kernel,
        name="pair_operators",
        out_shape=tuple(pltpu.VMEM(shape, F32) for shape in shapes),
        in_specs=[hbm, vmem, vmem],
        out_specs=(vmem, vmem, vmem),
        scratch_shapes=[
            pltpu.VMEM(tensor.shape, F32),
            pltpu.VMEM((16, subs, 64, 128), F32),
            pltpu.VMEM((groups, len(LEAVES), 2, 64, 128), F32),
            pltpu.VMEM((groups, 5, 256, 128), F32),
            pltpu.VMEM((groups, 5, 256, 128), F32),
            pltpu.VMEM((4, 8, 128), F32),
            pltpu.VMEM((4, 8, 128), F32),
            pltpu.VMEM((8, 32, 128), F32),
            pltpu.VMEM((2, 256, 128), F32),
            pltpu.VMEM((8, 8, 128), F32),
            pltpu.VMEM((2, 64, 128), F32),
            pltpu.VMEM((4, 64, 128), F32),
            pltpu.VMEM((64, 128), F32),
            pltpu.VMEM((5, 64, 256), BF16),
            pltpu.VMEM((512, 256), BF16),
            pltpu.VMEM((128, 128), F32),
            pltpu.VMEM((4, 16, 128), F32),
            pltpu.VMEM((4, 16, 128), F32),
            pltpu.VMEM((4, 16, 128), F32),
            pltpu.VMEM((4, 16, 128), F32),
            dma((groups,)),
            dma((groups,)),
            dma((groups,)),
            dma((groups, 5)),
            dma((groups, 5)),
            dma((35,)),
            dma((35,)),
            regular,
            regular,
        ],
        cost_estimate=pl.CostEstimate(flops=7 << 30, bytes_accessed=22 << 20, transcendentals=0),
        compiler_params=pltpu.CompilerParams(collective_id=0, has_side_effects=True, vmem_limit_bytes=44 << 20),
    )(tensor, two.T, three)
    return pl.pallas_call(
        keep,
        name="keep",
        out_shape=tuple(jax.ShapeDtypeStruct(shape, F32) for shape in shapes),
        in_specs=[vmem] * 3,
        out_specs=(hbm, hbm, hbm),
        scratch_shapes=[dma((13,))],
        compiler_params=pltpu.CompilerParams(vmem_limit_bytes=4 << 20),
    )(*results)


def solution(mesh):
    return jax.shard_map(
        per_device,
        mesh=mesh,
        in_specs=(P("gx", "gy", None), P("gy", "gx"), P(("gx", "gy"), None)),
        out_specs=(P("gx", "gy", None), P("gx", "gy", None), P("gx", None)),
        check_vma=False,
    )
```

```python
import functools

import jax
import jax.numpy as jnp
from jax import lax
from jax.experimental import pallas as pl
from jax.experimental.pallas import tpu as pltpu
from jax.sharding import PartitionSpec as P

MESH = pl.DeviceIdType.MESH
F32 = jnp.float32
BF16 = jnp.bfloat16
EAST, NORTH, WEST, SOUTH = range(4)

LEAVES = [
    ((EAST, EAST, NORTH, NORTH), NORTH),
    ((WEST, SOUTH), WEST),
    ((EAST, NORTH, NORTH), WEST),
    ((WEST, NORTH, NORTH), EAST),
    ((EAST, EAST, NORTH), SOUTH),
    ((WEST, NORTH), EAST),
    ((EAST, NORTH), SOUTH),
    ((EAST, SOUTH), NORTH),
    ((WEST,), EAST),
    ((SOUTH,), NORTH),
]
INNER = [
    ((EAST, EAST, SOUTH), (0, 1), (), NORTH),
    ((NORTH, NORTH), (2, 3), (), SOUTH),
    ((EAST, EAST), (4,), (0,), WEST),
    ((NORTH,), (5,), (1,), SOUTH),
    ((EAST,), (6, 7), (2,), WEST),
    ((), (8, 9), (4, 3), None),
]
STAGES = ((0, 1), (2, 3), (4,), (5,))
SKEW = 6
SUB = 4
ROWS = 8


def split(value):
    high = value.astype(BF16)
    return high, (value - high.astype(F32)).astype(BF16)


def kernel(
    tensor, two_hbm, three_hbm, pair_three, pair_two, mttkrp,
    whole, two, three, packed, raw, sent, got,
    tile_x, tile_y, tile_z, tile_c, col_z, col_c, near, two_own, weights, third, flip,
    local, sum_x, sum_y, total,
    load_sem, first_sem, raw_send, raw_recv, part_send, part_recv, gather_send, gather_recv, ready_z, ready_c,
    plane_send, plane_recv,
):
    gx, gy = lax.axis_index("gx"), lax.axis_index("gy")
    z, c = gx // 2, lax.rem(gx, 2)
    y, x = gy // 4, lax.rem(gy, 4)
    groups = whole.shape[0] // ROWS

    def at_x(step):
        return (gx, y * 4 + lax.rem(x + step, 4))

    def at_y(step):
        return (gx, lax.rem(y + step, 4) * 4 + x)

    def at_z(step):
        return (lax.rem(z + step, 8) * 2 + c, gy)

    at_c = (z * 2 + 1 - c, gy)

    def east_of(d):
        return (1 - d) * lax.rem(d + 1, 2)

    def north_of(d):
        return (2 - d) * lax.rem(d, 2)

    def turned(d, turn):
        return lax.rem(d + turn, 4)

    def beside(d):
        return (gx, lax.rem(y + north_of(d) + 4, 4) * 4 + lax.rem(x + east_of(d) + 4, 4))

    def block_of(place, turn):
        tx, ty = x + 8, y + 8
        for d in place:
            tx, ty = tx - east_of(turned(d, turn)), ty - north_of(turned(d, turn))
        return lax.rem(ty, 4) * 4 + lax.rem(tx, 4)

    def load(g):
        rows = pl.ds(g * ROWS, ROWS)
        return pltpu.make_async_copy(tensor.at[rows], whole.at[rows], load_sem.at[g])

    factor_loads = [
        pltpu.make_async_copy(three_hbm, three, first_sem.at[0]),
        pltpu.make_async_copy(two_hbm, two, first_sem.at[1]),
    ]
    for copy in factor_loads:
        copy.start()
    for g in range(groups):
        load(g).start()

    barrier = pltpu.get_barrier_semaphore()

    def greet(semaphore, device):
        pl.semaphore_signal(semaphore, inc=1, device_id=device, device_id_type=MESH)

    for s in (1, 2, 3):
        greet(barrier, at_x(s))
        greet(barrier, at_y(s))

    @pl.loop(z + 1, 8)
    def _(other):
        greet(barrier, (other * 2 + c, gy))

    @pl.when(c == 0)
    def _():
        greet(barrier, at_c)

    for copy in factor_loads:
        copy.wait()
    place = lax.broadcasted_iota(jnp.int32, (8, 128), 0)
    first, second = three[0:1, :], three[1:2, :]
    mine = jnp.where(place == 2 * x, first, jnp.where(place == 2 * x + 1, second, 0.0))
    tile_x[x] = mine
    flip[...] = jnp.zeros_like(flip)
    col_z[z] = jnp.zeros((8, 128), F32)
    col_z[z, :, 0:64] = two[...]

    pl.semaphore_wait(barrier, 6 + z + c)

    @pl.loop(0, z)
    def _(other):
        greet(ready_z, (other * 2 + c, gy))

    @pl.when(c == 1)
    def _():
        greet(ready_c, at_c)

    def gather(slot, ref, own, dst, device):
        return pltpu.make_async_remote_copy(
            src_ref=ref.at[own],
            dst_ref=ref.at[dst],
            send_sem=gather_send.at[slot],
            recv_sem=gather_recv.at[slot],
            device_id=device,
            device_id_type=MESH,
        )

    def ring(slot, ref, own, size, device):
        return [gather(slot + s - 1, ref, own, own, device(s)) for s in range(1, size)]

    three_x = ring(0, tile_x, x, 4, at_x)
    three_y = ring(3, tile_y, y, 4, at_y)
    three_z = ring(6, tile_z, z, 8, at_z)
    three_c = [gather(13, tile_c, c, c, at_c)]

    def two_z(other):
        return pltpu.make_async_remote_copy(
            src_ref=col_z.at[z],
            dst_ref=col_z.at[z],
            send_sem=plane_send.at[other],
            recv_sem=plane_recv.at[z],
            device_id=(other * 2 + c, gy),
            device_id_type=MESH,
        )

    def from_plane(other):
        pltpu.make_async_copy(col_z.at[other], col_z.at[other], plane_send.at[other]).wait()
        pltpu.make_async_copy(col_z.at[other], col_z.at[other], plane_recv.at[other]).wait()

    two_c = [gather(21, col_c, c, c, at_c)]
    two_near = [
        pltpu.make_async_remote_copy(
            src_ref=two_own,
            dst_ref=near.at[(d + 2) % 4],
            send_sem=gather_send.at[22 + d],
            recv_sem=gather_recv.at[22 + d],
            device_id=beside(d),
            device_id_type=MESH,
        )
        for d in range(4)
    ]
    sum_one = [
        pltpu.make_async_remote_copy(
            src_ref=local.at[lax.rem(x + s, 4)],
            dst_ref=sum_x.at[x],
            send_sem=gather_send.at[25 + s],
            recv_sem=gather_recv.at[25 + s],
            device_id=at_x(s),
            device_id_type=MESH,
        )
        for s in (1, 2, 3)
    ]
    sum_two = ring(29, sum_y, y, 4, at_y)
    sum_three = ring(32, total, x, 4, at_x)

    def start(copies):
        for copy in copies:
            copy.start()

    def finish(copies):
        for copy in copies:
            copy.wait()

    start(three_x)

    @pl.loop(0, z)
    def _(other):
        two_z(other).start()

    lane = lax.broadcasted_iota(jnp.int32, (64, 128), 1)
    low_half = lane < 64
    even = lax.rem(lane // 32, 2) == 0

    def pack(s):
        for quarter in range(4):
            a = [whole[s * SUB + i, :, pl.ds(quarter * 128, 128)] for i in range(SUB)]
            left = [jnp.where(low_half, a[i], pltpu.roll(a[i + 2], 64, 1)) for i in (0, 1)]
            right = [jnp.where(low_half, pltpu.roll(a[i], 64, 1), a[i + 2]) for i in (0, 1)]
            for half, (p, q) in enumerate((left, right)):
                packed[quarter * 4 + half * 2, s] = jnp.where(even, p, pltpu.roll(q, 32, 1))
                packed[quarter * 4 + half * 2 + 1, s] = jnp.where(even, pltpu.roll(p, 96, 1), q)

    def send_leaf(g, turn, n):
        place, d = LEAVES[n]
        return pltpu.make_async_remote_copy(
            src_ref=packed.at[block_of(place, turn), pl.ds(2 * g, 2)],
            dst_ref=raw.at[g, n],
            send_sem=raw_send.at[g],
            recv_sem=raw_recv.at[g],
            device_id=beside(turned(d, turn)),
            device_id_type=MESH,
        )

    @pl.loop(0, groups)
    def _(g):
        turn = lax.rem(g, 4)
        load(g).wait()
        pack(2 * g)
        pack(2 * g + 1)
        for n in range(len(LEAVES)):
            send_leaf(g, turn, n).start()

        @pl.when(g == 1)
        def _():
            finish(three_x)
            tile_y[y] = tile_x[0] + tile_x[1] + tile_x[2] + tile_x[3]
            start(three_y)

        @pl.when(g == 3)
        def _():
            @pl.when(z < 7)
            def _():
                pl.semaphore_wait(ready_z, 7 - z)

            @pl.loop(z + 1, 8)
            def _(other):
                two_z(other).start()

            finish(three_y)
            for k in range(4):
                tile_z[z, pl.ds(8 * k, 8), :] = tile_y[k]
            start(three_z)

        @pl.when(g == 4)
        def _():
            pl.loop(0, z)(from_plane)
            pl.loop(z + 1, 8)(from_plane)
            for k in range(8):
                col_c[c, pl.ds(8 * k, 8), :] = col_z[k]

            @pl.when(c == 0)
            def _():
                pl.semaphore_wait(ready_c, 1)

            start(two_c)

        @pl.when(g == 5)
        def _():
            finish(two_c)
            for k in range(8):
                for core in range(2):
                    flip[pl.ds(16 * k + 8 * core, 8), :] = col_c[core, pl.ds(8 * k, 8), :]
            two_own[...] = jnp.transpose(flip[...])[0:64, :]
            start(two_near)

    finish(three_z)
    for k in range(8):
        tile_c[c, pl.ds(32 * k, 32), :] = tile_z[k]
    start(three_c)
    finish(three_c)
    for k in range(8):
        for core in range(2):
            high, low = split(tile_c[core, pl.ds(32 * k, 32), :])
            third[pl.ds(64 * k + 32 * core, 32), 0:128] = high
            third[pl.ds(64 * k + 32 * core, 32), 128:256] = low

    def times(value, weight, contract):
        dims = (((contract,), (0,)), ((), ()))
        out = sum(lax.dot_general(part, weight, dims, preferred_element_type=F32) for part in split(value))
        return out[:, 0:128] + out[:, 128:256]

    def contract_third(g):
        for i in range(0, ROWS, 2):
            rows = pl.ds(g * ROWS + i, 2)
            result = times(whole[rows].reshape(128, 512), third[...], 1).reshape(2, 64, 128)
            pair_three[rows] = result
            sums = jnp.sum(result * two_own[...][None], axis=1)
            local[g // 2, pl.ds(lax.rem(g, 2) * 8 + i, 2), :] = sums

    def send_part(g, turn, n):
        return pltpu.make_async_remote_copy(
            src_ref=sent.at[g, n],
            dst_ref=got.at[g, n],
            send_sem=part_send.at[g, n],
            recv_sem=part_recv.at[g, n],
            device_id=beside(turned(INNER[n][3], turn)),
            device_id_type=MESH,
        )

    def inner(g, n):
        turn = lax.rem(g, 4)
        place, leaves, parts, d = INNER[n]
        own = block_of(place, turn)
        pieces, weight = [[packed[own, 2 * g + h] for h in (0, 1)]], [weights[4]]
        for leaf in leaves:
            pieces.append([raw[g, leaf, h] for h in (0, 1)])
            weight.append(weights[turned((LEAVES[leaf][1] + 2) % 4, turn)])
        stacked = jnp.concatenate([jnp.concatenate(piece, axis=1) for piece in pieces], axis=0)
        result = times(stacked, jnp.concatenate(weight, axis=0), 0)
        for part in parts:
            pltpu.make_async_copy(got.at[g, part], got.at[g, part], part_recv.at[g, part]).wait()
            result = result + got[g, part]
        if d is None:
            pair_two[pl.ds(g * ROWS, ROWS)] = result.reshape(ROWS, 32, 128)
        else:
            sent[g, n] = result
            send_part(g, turn, n).start()

    pl.loop(0, groups)(contract_third)
    sum_x[x] = local[x]
    start(sum_one)

    finish(two_near)
    for k in range(5):
        high, low = split(two_own[...] if k == 4 else near[k])
        weights[k, :, 0:128] = high
        weights[k, :, 128:256] = low

    @pl.loop(0, groups + 3 * SKEW)
    def _(step):
        @pl.when(step < groups)
        def _():
            pltpu.make_async_copy(raw.at[step], raw.at[step], raw_recv.at[step]).wait()

        for late, nodes in enumerate(STAGES):
            g = step - late * SKEW

            @pl.when((g >= 0) & (g < groups))
            def _(g=g, nodes=nodes):
                for n in nodes:
                    inner(g, n)

        @pl.when(step == groups)
        def _():
            finish(sum_one)
            sum_y[y] = sum_x[0] + sum_x[1] + sum_x[2] + sum_x[3]
            start(sum_two)

        @pl.when(step == groups + 6)
        def _():
            finish(sum_two)
            total[x] = sum_y[0] + sum_y[1] + sum_y[2] + sum_y[3]
            start(sum_three)

    finish(sum_three)
    for k in range(4):
        mttkrp[pl.ds(16 * k, 16), :] = total[k]

    @pl.loop(0, groups)
    def _(g):
        pltpu.make_async_copy(raw.at[g], raw.at[g], raw_send.at[g]).wait()
        for n in range(5):
            pltpu.make_async_copy(sent.at[g, n], sent.at[g, n], part_send.at[g, n]).wait()


def keep(*refs):
    sources, targets, sem = refs[:3], refs[3:6], refs[6]
    copies = []
    for source, target, parts in zip(sources, targets, (8, 4, 1)):
        size = source.shape[0] // parts
        for n in range(parts):
            rows = pl.ds(n * size, size)
            copies.append(pltpu.make_async_copy(source.at[rows], target.at[rows], sem.at[len(copies)]))
    for copy in copies:
        copy.start()
    for copy in copies:
        copy.wait()


def per_device(tensor, two, three):
    rows = tensor.shape[0]
    groups, subs = rows // ROWS, rows // SUB
    shapes = ((rows, 64, 128), (rows, 32, 128), (rows, 128))
    hbm, vmem = pl.BlockSpec(memory_space=pl.ANY), pl.BlockSpec(memory_space=pltpu.VMEM)
    dma, regular = pltpu.SemaphoreType.DMA, pltpu.SemaphoreType.REGULAR
    results = pl.pallas_call(
        kernel,
        name="pair_operators",
        out_shape=tuple(pltpu.VMEM(shape, F32) for shape in shapes),
        in_specs=[hbm, pl.BlockSpec(memory_space=pltpu.HBM), pl.BlockSpec(memory_space=pltpu.HBM)],
        out_specs=(vmem, vmem, vmem),
        scratch_shapes=[
            pltpu.VMEM(tensor.shape, F32),
            pltpu.VMEM((8, 64), F32),
            pltpu.VMEM((2, 128), F32),
            pltpu.VMEM((16, subs, 64, 128), F32),
            pltpu.VMEM((groups, len(LEAVES), 2, 64, 128), F32),
            pltpu.VMEM((groups, 5, 256, 128), F32),
            pltpu.VMEM((groups, 5, 256, 128), F32),
            pltpu.VMEM((4, 8, 128), F32),
            pltpu.VMEM((4, 8, 128), F32),
            pltpu.VMEM((8, 32, 128), F32),
            pltpu.VMEM((2, 256, 128), F32),
            pltpu.VMEM((8, 8, 128), F32),
            pltpu.VMEM((2, 64, 128), F32),
            pltpu.VMEM((4, 64, 128), F32),
            pltpu.VMEM((64, 128), F32),
            pltpu.VMEM((5, 64, 256), BF16),
            pltpu.VMEM((512, 256), BF16),
            pltpu.VMEM((128, 128), F32),
            pltpu.VMEM((4, 16, 128), F32),
            pltpu.VMEM((4, 16, 128), F32),
            pltpu.VMEM((4, 16, 128), F32),
            pltpu.VMEM((4, 16, 128), F32),
            dma((groups,)),
            dma((2,)),
            dma((groups,)),
            dma((groups,)),
            dma((groups, 5)),
            dma((groups, 5)),
            dma((35,)),
            dma((35,)),
            regular,
            regular,
            dma((8,)),
            dma((8,)),
        ],
        cost_estimate=pl.CostEstimate(flops=7 << 30, bytes_accessed=22 << 20, transcendentals=0),
        compiler_params=pltpu.CompilerParams(collective_id=0, has_side_effects=True, vmem_limit_bytes=44 << 20),
    )(tensor, pltpu.with_memory_space_constraint(two.T, pltpu.HBM), pltpu.with_memory_space_constraint(three, pltpu.HBM))
    return pl.pallas_call(
        keep,
        name="keep",
        out_shape=tuple(jax.ShapeDtypeStruct(shape, F32) for shape in shapes),
        in_specs=[vmem] * 3,
        out_specs=(hbm, hbm, hbm),
        scratch_shapes=[dma((13,))],
        compiler_params=pltpu.CompilerParams(vmem_limit_bytes=4 << 20),
    )(*results)


def solution(mesh):
    return jax.shard_map(
        per_device,
        mesh=mesh,
        in_specs=(P("gx", "gy", None), P("gy", "gx"), P(("gx", "gy"), None)),
        out_specs=(P("gx", "gy", None), P("gx", "gy", None), P("gx", None)),
        check_vma=False,
    )
```

```python
import functools

import jax
import jax.numpy as jnp
from jax import lax
from jax.experimental import pallas as pl
from jax.experimental.pallas import tpu as pltpu
from jax.sharding import PartitionSpec as P

MESH = pl.DeviceIdType.MESH
F32 = jnp.float32
BF16 = jnp.bfloat16
EAST, NORTH, WEST, SOUTH = range(4)

LEAVES = [
    ((EAST, EAST, NORTH, NORTH), NORTH),
    ((WEST, SOUTH), WEST),
    ((EAST, NORTH, NORTH), WEST),
    ((WEST, NORTH, NORTH), EAST),
    ((EAST, EAST, NORTH), SOUTH),
    ((WEST, NORTH), EAST),
    ((EAST, NORTH), SOUTH),
    ((EAST, SOUTH), NORTH),
    ((WEST,), EAST),
    ((SOUTH,), NORTH),
]
INNER = [
    ((EAST, EAST, SOUTH), (0, 1), (), NORTH),
    ((NORTH, NORTH), (2, 3), (), SOUTH),
    ((EAST, EAST), (4,), (0,), WEST),
    ((NORTH,), (5,), (1,), SOUTH),
    ((EAST,), (6, 7), (2,), WEST),
    ((), (8, 9), (4, 3), None),
]
STAGES = ((0, 1), (2, 3), (4,), (5,))
SKEW = 7
SUB = 4
ROWS = 8


def split(value):
    high = value.astype(BF16)
    return high, (value - high.astype(F32)).astype(BF16)


def kernel(
    tensor, two_hbm, three_hbm, pair_three, pair_two, mttkrp,
    whole, two, three, packed, raw, sent, got,
    tile_x, tile_y, tile_z, tile_c, col_z, col_c, near, two_own, weights, third, flip,
    local, sum_x, sum_y, total,
    load_sem, first_sem, raw_send, raw_recv, part_send, part_recv, gather_send, gather_recv, ready_z, ready_c,
    plane_send, plane_recv,
):
    gx, gy = lax.axis_index("gx"), lax.axis_index("gy")
    z, c = gx // 2, lax.rem(gx, 2)
    y, x = gy // 4, lax.rem(gy, 4)
    groups = whole.shape[0] // ROWS

    def at_x(step):
        return (gx, y * 4 + lax.rem(x + step, 4))

    def at_y(step):
        return (gx, lax.rem(y + step, 4) * 4 + x)

    def at_z(step):
        return (lax.rem(z + step, 8) * 2 + c, gy)

    at_c = (z * 2 + 1 - c, gy)

    def east_of(d):
        return (1 - d) * lax.rem(d + 1, 2)

    def north_of(d):
        return (2 - d) * lax.rem(d, 2)

    def turned(d, turn):
        return lax.rem(d + turn, 4)

    def beside(d):
        return (gx, lax.rem(y + north_of(d) + 4, 4) * 4 + lax.rem(x + east_of(d) + 4, 4))

    def block_of(place, turn):
        tx, ty = x + 8, y + 8
        for d in place:
            tx, ty = tx - east_of(turned(d, turn)), ty - north_of(turned(d, turn))
        return lax.rem(ty, 4) * 4 + lax.rem(tx, 4)

    def load(g):
        rows = pl.ds(g * ROWS, ROWS)
        return pltpu.make_async_copy(tensor.at[rows], whole.at[rows], load_sem.at[g])

    factor_loads = [
        pltpu.make_async_copy(three_hbm, three, first_sem.at[0]),
        pltpu.make_async_copy(two_hbm, two, first_sem.at[1]),
    ]
    for copy in factor_loads:
        copy.start()
    load(0).start()

    barrier = pltpu.get_barrier_semaphore()

    def greet(semaphore, device):
        pl.semaphore_signal(semaphore, inc=1, device_id=device, device_id_type=MESH)

    for s in (1, 2, 3):
        greet(barrier, at_x(s))
        greet(barrier, at_y(s))

    @pl.loop(z + 1, 8)
    def _(other):
        greet(barrier, (other * 2 + c, gy))

    @pl.when(c == 0)
    def _():
        greet(barrier, at_c)

    lane = lax.broadcasted_iota(jnp.int32, (64, 128), 1)
    low_half = lane < 64
    even = lax.rem(lane // 32, 2) == 0

    def pack(s):
        for quarter in range(4):
            a = [whole[s * SUB + i, :, pl.ds(quarter * 128, 128)] for i in range(SUB)]
            left = [jnp.where(low_half, a[i], pltpu.roll(a[i + 2], 64, 1)) for i in (0, 1)]
            right = [jnp.where(low_half, pltpu.roll(a[i], 64, 1), a[i + 2]) for i in (0, 1)]
            for half, (p, q) in enumerate((left, right)):
                packed[quarter * 4 + half * 2, s] = jnp.where(even, p, pltpu.roll(q, 32, 1))
                packed[quarter * 4 + half * 2 + 1, s] = jnp.where(even, pltpu.roll(p, 96, 1), q)

    for copy in factor_loads:
        copy.wait()
    place = lax.broadcasted_iota(jnp.int32, (8, 128), 0)
    first, second = three[0:1, :], three[1:2, :]
    mine = jnp.where(place == 2 * x, first, jnp.where(place == 2 * x + 1, second, 0.0))
    tile_x[x] = mine
    flip[...] = jnp.zeros_like(flip)
    col_z[z] = jnp.zeros((8, 128), F32)
    col_z[z, :, 0:64] = two[...]

    for g in range(1, groups):
        load(g).start()
    load(0).wait()
    pack(0)
    pack(1)
    pl.semaphore_wait(barrier, 6 + z + c)

    def gather(slot, ref, own, dst, device):
        return pltpu.make_async_remote_copy(
            src_ref=ref.at[own],
            dst_ref=ref.at[dst],
            send_sem=gather_send.at[slot],
            recv_sem=gather_recv.at[slot],
            device_id=device,
            device_id_type=MESH,
        )

    def ring(slot, ref, own, size, device):
        return [gather(slot + s - 1, ref, own, own, device(s)) for s in range(1, size)]

    three_x = ring(0, tile_x, x, 4, at_x)
    three_y = ring(3, tile_y, y, 4, at_y)
    three_z = ring(6, tile_z, z, 8, at_z)
    three_c = [gather(13, tile_c, c, c, at_c)]

    def two_z(other):
        return pltpu.make_async_remote_copy(
            src_ref=col_z.at[z],
            dst_ref=col_z.at[z],
            send_sem=plane_send.at[other],
            recv_sem=plane_recv.at[z],
            device_id=(other * 2 + c, gy),
            device_id_type=MESH,
        )

    def from_plane(other):
        pltpu.make_async_copy(col_z.at[other], col_z.at[other], plane_send.at[other]).wait()
        pltpu.make_async_copy(col_z.at[other], col_z.at[other], plane_recv.at[other]).wait()

    two_c = [gather(21, col_c, c, c, at_c)]
    half = pl.ds(32 * c, 32)
    near_c = pltpu.make_async_remote_copy(
        src_ref=near.at[:, half],
        dst_ref=near.at[:, half],
        send_sem=gather_send.at[14],
        recv_sem=gather_recv.at[14],
        device_id=at_c,
        device_id_type=MESH,
    )
    two_near = [
        pltpu.make_async_remote_copy(
            src_ref=two_own.at[half],
            dst_ref=near.at[(d + 2) % 4, half],
            send_sem=gather_send.at[22 + d],
            recv_sem=gather_recv.at[22 + d],
            device_id=beside(d),
            device_id_type=MESH,
        )
        for d in range(4)
    ]
    sum_one = [
        pltpu.make_async_remote_copy(
            src_ref=local.at[lax.rem(x + s, 4)],
            dst_ref=sum_x.at[x],
            send_sem=gather_send.at[25 + s],
            recv_sem=gather_recv.at[25 + s],
            device_id=at_x(s),
            device_id_type=MESH,
        )
        for s in (1, 2, 3)
    ]
    sum_two = ring(29, sum_y, y, 4, at_y)
    sum_three = ring(32, total, x, 4, at_x)

    def start(copies):
        for copy in copies:
            copy.start()

    def finish(copies):
        for copy in copies:
            copy.wait()

    start(three_x)

    def send_leaf(g, turn, n):
        place, d = LEAVES[n]
        return pltpu.make_async_remote_copy(
            src_ref=packed.at[block_of(place, turn), pl.ds(2 * g, 2)],
            dst_ref=raw.at[g, n],
            send_sem=raw_send,
            recv_sem=raw_recv.at[g],
            device_id=beside(turned(d, turn)),
            device_id_type=MESH,
        )

    @pl.loop(0, groups)
    def _(g):
        turn = lax.rem(g, 4)
        for n in range(len(LEAVES)):
            send_leaf(g, turn, n).start()

        @pl.when(g == 0)
        def _():
            @pl.loop(0, z)
            def _(other):
                greet(ready_z, (other * 2 + c, gy))

            @pl.when(c == 1)
            def _():
                greet(ready_c, at_c)

            @pl.loop(0, z)
            def _(other):
                two_z(other).start()

        @pl.when(g == 1)
        def _():
            finish(three_x)
            tile_y[y] = tile_x[0] + tile_x[1] + tile_x[2] + tile_x[3]
            start(three_y)

        @pl.when(g == 3)
        def _():
            @pl.when(z < 7)
            def _():
                pl.semaphore_wait(ready_z, 7 - z)

            @pl.loop(z + 1, 8)
            def _(other):
                two_z(other).start()

            finish(three_y)
            for k in range(4):
                tile_z[z, pl.ds(8 * k, 8), :] = tile_y[k]
            start(three_z)

        @pl.when(g == 4)
        def _():
            pl.loop(0, z)(from_plane)
            pl.loop(z + 1, 8)(from_plane)
            for k in range(8):
                col_c[c, pl.ds(8 * k, 8), :] = col_z[k]

            @pl.when(c == 0)
            def _():
                pl.semaphore_wait(ready_c, 1)

            start(two_c)

        @pl.when(g == 5)
        def _():
            finish(two_c)
            for k in range(8):
                for core in range(2):
                    flip[pl.ds(16 * k + 8 * core, 8), :] = col_c[core, pl.ds(8 * k, 8), :]
            two_own[...] = jnp.transpose(flip[...])[0:64, :]
            start(two_near)

        @pl.when(g < groups - 1)
        def _():
            load(g + 1).wait()
            pack(2 * g + 2)
            pack(2 * g + 3)

    finish(three_z)
    for k in range(8):
        tile_c[c, pl.ds(32 * k, 32), :] = tile_z[k]
    start(three_c)
    finish(three_c)
    for k in range(8):
        for core in range(2):
            high, low = split(tile_c[core, pl.ds(32 * k, 32), :])
            third[pl.ds(64 * k + 32 * core, 32), 0:128] = high
            third[pl.ds(64 * k + 32 * core, 32), 128:256] = low

    def times(value, weight, contract):
        dims = (((contract,), (0,)), ((), ()))
        out = sum(lax.dot_general(part, weight, dims, preferred_element_type=F32) for part in split(value))
        return out[:, 0:128] + out[:, 128:256]

    def contract_third(g):
        for i in range(0, ROWS, 2):
            rows = pl.ds(g * ROWS + i, 2)
            result = times(whole[rows].reshape(128, 512), third[...], 1).reshape(2, 64, 128)
            pair_three[rows] = result
            sums = jnp.sum(result * two_own[...][None], axis=1)
            local[g // 2, pl.ds(lax.rem(g, 2) * 8 + i, 2), :] = sums

    def send_part(g, turn, n):
        return pltpu.make_async_remote_copy(
            src_ref=sent.at[g, n],
            dst_ref=got.at[g, n],
            send_sem=part_send,
            recv_sem=part_recv.at[g, n],
            device_id=beside(turned(INNER[n][3], turn)),
            device_id_type=MESH,
        )

    def inner(g, n):
        turn = lax.rem(g, 4)
        place, leaves, parts, d = INNER[n]
        own = block_of(place, turn)
        pieces, weight = [[packed[own, 2 * g + h] for h in (0, 1)]], [weights[4]]
        for leaf in leaves:
            pieces.append([raw[g, leaf, h] for h in (0, 1)])
            weight.append(weights[turned((LEAVES[leaf][1] + 2) % 4, turn)])
        stacked = jnp.concatenate([jnp.concatenate(piece, axis=1) for piece in pieces], axis=0)
        result = times(stacked, jnp.concatenate(weight, axis=0), 0)
        for part in parts:
            pltpu.make_async_copy(got.at[g, part], got.at[g, part], part_recv.at[g, part]).wait()
            result = result + got[g, part]
        if d is None:
            pair_two[pl.ds(g * ROWS, ROWS)] = result.reshape(ROWS, 32, 128)
        else:
            sent[g, n] = result
            send_part(g, turn, n).start()

    pl.loop(0, groups // 2)(contract_third)
    finish(two_near)
    near_c.start()
    pl.loop(groups // 2, groups)(contract_third)
    sum_x[x] = local[x]
    start(sum_one)
    near_c.wait()
    for k in range(5):
        high, low = split(two_own[...] if k == 4 else near[k])
        weights[k, :, 0:128] = high
        weights[k, :, 128:256] = low

    @pl.loop(0, groups + 3 * SKEW)
    def _(step):
        @pl.when(step < groups)
        def _():
            pltpu.make_async_copy(raw.at[step], raw.at[step], raw_recv.at[step]).wait()

        for late, nodes in enumerate(STAGES):
            g = step - late * SKEW

            @pl.when((g >= 0) & (g < groups))
            def _(g=g, nodes=nodes):
                for n in nodes:
                    inner(g, n)

        @pl.when(step == groups)
        def _():
            finish(sum_one)
            sum_y[y] = sum_x[0] + sum_x[1] + sum_x[2] + sum_x[3]
            start(sum_two)

        @pl.when(step == groups + 6)
        def _():
            finish(sum_two)
            total[x] = sum_y[0] + sum_y[1] + sum_y[2] + sum_y[3]
            start(sum_three)

    finish(sum_three)
    for k in range(4):
        mttkrp[pl.ds(16 * k, 16), :] = total[k]

    pltpu.make_async_copy(raw, raw, raw_send).wait()
    pltpu.make_async_copy(sent, sent, part_send).wait()


def keep(*refs):
    sources, targets, sem = refs[:3], refs[3:6], refs[6]
    copies = []
    for source, target, parts in zip(sources, targets, (8, 4, 1)):
        size = source.shape[0] // parts
        for n in range(parts):
            rows = pl.ds(n * size, size)
            copies.append(pltpu.make_async_copy(source.at[rows], target.at[rows], sem.at[len(copies)]))
    for copy in copies:
        copy.start()
    for copy in copies:
        copy.wait()


def per_device(tensor, two, three):
    rows = tensor.shape[0]
    groups, subs = rows // ROWS, rows // SUB
    shapes = ((rows, 64, 128), (rows, 32, 128), (rows, 128))
    hbm, vmem = pl.BlockSpec(memory_space=pl.ANY), pl.BlockSpec(memory_space=pltpu.VMEM)
    dma, regular = pltpu.SemaphoreType.DMA, pltpu.SemaphoreType.REGULAR
    results = pl.pallas_call(
        kernel,
        name="pair_operators",
        out_shape=tuple(pltpu.VMEM(shape, F32) for shape in shapes),
        in_specs=[hbm, pl.BlockSpec(memory_space=pltpu.HBM), pl.BlockSpec(memory_space=pltpu.HBM)],
        out_specs=(vmem, vmem, vmem),
        scratch_shapes=[
            pltpu.VMEM(tensor.shape, F32),
            pltpu.VMEM((8, 64), F32),
            pltpu.VMEM((2, 128), F32),
            pltpu.VMEM((16, subs, 64, 128), F32),
            pltpu.VMEM((groups, len(LEAVES), 2, 64, 128), F32),
            pltpu.VMEM((groups, 5, 256, 128), F32),
            pltpu.VMEM((groups, 5, 256, 128), F32),
            pltpu.VMEM((4, 8, 128), F32),
            pltpu.VMEM((4, 8, 128), F32),
            pltpu.VMEM((8, 32, 128), F32),
            pltpu.VMEM((2, 256, 128), F32),
            pltpu.VMEM((8, 8, 128), F32),
            pltpu.VMEM((2, 64, 128), F32),
            pltpu.VMEM((4, 64, 128), F32),
            pltpu.VMEM((64, 128), F32),
            pltpu.VMEM((5, 64, 256), BF16),
            pltpu.VMEM((512, 256), BF16),
            pltpu.VMEM((128, 128), F32),
            pltpu.VMEM((4, 16, 128), F32),
            pltpu.VMEM((4, 16, 128), F32),
            pltpu.VMEM((4, 16, 128), F32),
            pltpu.VMEM((4, 16, 128), F32),
            dma((groups,)),
            dma((2,)),
            dma,
            dma((groups,)),
            dma,
            dma((groups, 5)),
            dma((35,)),
            dma((35,)),
            regular,
            regular,
            dma((8,)),
            dma((8,)),
        ],
        cost_estimate=pl.CostEstimate(flops=7 << 30, bytes_accessed=22 << 20, transcendentals=0),
        compiler_params=pltpu.CompilerParams(collective_id=0, has_side_effects=True, vmem_limit_bytes=44 << 20),
    )(tensor, pltpu.with_memory_space_constraint(two.T, pltpu.HBM), pltpu.with_memory_space_constraint(three, pltpu.HBM))
    return pl.pallas_call(
        keep,
        name="keep",
        out_shape=tuple(jax.ShapeDtypeStruct(shape, F32) for shape in shapes),
        in_specs=[vmem] * 3,
        out_specs=(hbm, hbm, hbm),
        scratch_shapes=[dma((13,))],
        compiler_params=pltpu.CompilerParams(vmem_limit_bytes=4 << 20),
    )(*results)


def solution(mesh):
    return jax.shard_map(
        per_device,
        mesh=mesh,
        in_specs=(P("gx", "gy", None), P("gy", "gx"), P(("gx", "gy"), None)),
        out_specs=(P("gx", "gy", None), P("gx", "gy", None), P("gx", None)),
        check_vma=False,
    )
```

```python
import functools

import jax
import jax.numpy as jnp
from jax import lax
from jax.experimental import pallas as pl
from jax.experimental.pallas import tpu as pltpu
from jax.sharding import PartitionSpec as P

MESH = pl.DeviceIdType.MESH
F32 = jnp.float32
BF16 = jnp.bfloat16
EAST, NORTH, WEST, SOUTH = range(4)

LEAVES = [
    ((EAST, EAST, NORTH, NORTH), NORTH),
    ((WEST, SOUTH), WEST),
    ((EAST, NORTH, NORTH), WEST),
    ((WEST, NORTH, NORTH), EAST),
    ((EAST, EAST, NORTH), SOUTH),
    ((WEST, NORTH), EAST),
    ((EAST, NORTH), SOUTH),
    ((EAST, SOUTH), NORTH),
    ((WEST,), EAST),
    ((SOUTH,), NORTH),
]
INNER = [
    ((EAST, EAST, SOUTH), (0, 1), (), NORTH),
    ((NORTH, NORTH), (2, 3), (), SOUTH),
    ((EAST, EAST), (4,), (0,), WEST),
    ((NORTH,), (5,), (1,), SOUTH),
    ((EAST,), (6, 7), (2,), WEST),
    ((), (8, 9), (4, 3), None),
]
STAGES = ((0, 1), (2, 3), (4,), (5,))
SKEW = 7
SUB = 4
ROWS = 8


def split(value):
    high = value.astype(BF16)
    return high, (value - high.astype(F32)).astype(BF16)


def kernel(
    tensor, two_hbm, three_hbm, pair_three, pair_two, mttkrp,
    whole, two, three, packed, raw, sent, got,
    tile_x, tile_y, tile_z, tile_c, col_z, col_c, near, two_own, weights, third, flip,
    local, sum_x, sum_y, total,
    load_sem, first_sem, raw_send, raw_recv, part_send, part_recv, gather_send, gather_recv, ready_z, ready_c,
    plane_send, plane_recv,
):
    gx, gy = lax.axis_index("gx"), lax.axis_index("gy")
    z, c = gx // 2, lax.rem(gx, 2)
    y, x = gy // 4, lax.rem(gy, 4)
    groups = whole.shape[0] // ROWS

    def at_x(step):
        return (gx, y * 4 + lax.rem(x + step, 4))

    def at_y(step):
        return (gx, lax.rem(y + step, 4) * 4 + x)

    def at_z(step):
        return (lax.rem(z + step, 8) * 2 + c, gy)

    at_c = (z * 2 + 1 - c, gy)

    def east_of(d):
        return (1 - d) * lax.rem(d + 1, 2)

    def north_of(d):
        return (2 - d) * lax.rem(d, 2)

    def turn_of(g):
        return lax.rem(2 * lax.rem(g, 2) + lax.rem(g // 2, 2) + 2 * c, 4)

    def turned(d, turn):
        return lax.rem(d + turn, 4)

    def beside(d):
        return (gx, lax.rem(y + north_of(d) + 4, 4) * 4 + lax.rem(x + east_of(d) + 4, 4))

    def block_of(place, turn):
        tx, ty = x + 8, y + 8
        for d in place:
            tx, ty = tx - east_of(turned(d, turn)), ty - north_of(turned(d, turn))
        return lax.rem(ty, 4) * 4 + lax.rem(tx, 4)

    def load(g):
        rows = pl.ds(g * ROWS, ROWS)
        return pltpu.make_async_copy(tensor.at[rows], whole.at[rows], load_sem.at[g])

    factor_loads = [
        pltpu.make_async_copy(three_hbm, three, first_sem.at[0]),
        pltpu.make_async_copy(two_hbm, two, first_sem.at[1]),
    ]
    for copy in factor_loads:
        copy.start()
    load(0).start()

    barrier = pltpu.get_barrier_semaphore()

    def greet(semaphore, device):
        pl.semaphore_signal(semaphore, inc=1, device_id=device, device_id_type=MESH)

    for s in (1, 2, 3):
        greet(barrier, at_x(s))
        greet(barrier, at_y(s))

    @pl.loop(z + 1, 8)
    def _(other):
        greet(barrier, (other * 2 + c, gy))

    @pl.when(c == 0)
    def _():
        greet(barrier, at_c)

    lane = lax.broadcasted_iota(jnp.int32, (64, 128), 1)
    low_half = lane < 64
    even = lax.rem(lane // 32, 2) == 0

    def pack(s):
        for quarter in range(4):
            a = [whole[s * SUB + i, :, pl.ds(quarter * 128, 128)] for i in range(SUB)]
            left = [jnp.where(low_half, a[i], pltpu.roll(a[i + 2], 64, 1)) for i in (0, 1)]
            right = [jnp.where(low_half, pltpu.roll(a[i], 64, 1), a[i + 2]) for i in (0, 1)]
            for half, (p, q) in enumerate((left, right)):
                packed[quarter * 4 + half * 2, s] = jnp.where(even, p, pltpu.roll(q, 32, 1))
                packed[quarter * 4 + half * 2 + 1, s] = jnp.where(even, pltpu.roll(p, 96, 1), q)

    for copy in factor_loads:
        copy.wait()
    place = lax.broadcasted_iota(jnp.int32, (8, 128), 0)
    first, second = three[0:1, :], three[1:2, :]
    mine = jnp.where(place == 2 * x, first, jnp.where(place == 2 * x + 1, second, 0.0))
    tile_x[x] = mine
    flip[...] = jnp.zeros_like(flip)
    col_z[z] = jnp.zeros((8, 128), F32)
    col_z[z, :, 0:64] = two[...]

    for g in range(1, groups):
        load(g).start()
    load(0).wait()
    pack(0)
    pack(1)
    pl.semaphore_wait(barrier, 6 + z + c)

    def gather(slot, ref, own, dst, device):
        return pltpu.make_async_remote_copy(
            src_ref=ref.at[own],
            dst_ref=ref.at[dst],
            send_sem=gather_send.at[slot],
            recv_sem=gather_recv.at[slot],
            device_id=device,
            device_id_type=MESH,
        )

    def ring(slot, ref, own, size, device):
        return [gather(slot + s - 1, ref, own, own, device(s)) for s in range(1, size)]

    three_x = ring(0, tile_x, x, 4, at_x)
    three_y = ring(3, tile_y, y, 4, at_y)
    three_z = ring(6, tile_z, z, 8, at_z)
    three_c = [gather(13, tile_c, c, c, at_c)]

    def two_z(other):
        return pltpu.make_async_remote_copy(
            src_ref=col_z.at[z],
            dst_ref=col_z.at[z],
            send_sem=plane_send.at[other],
            recv_sem=plane_recv.at[z],
            device_id=(other * 2 + c, gy),
            device_id_type=MESH,
        )

    def from_plane(other):
        pltpu.make_async_copy(col_z.at[other], col_z.at[other], plane_send.at[other]).wait()
        pltpu.make_async_copy(col_z.at[other], col_z.at[other], plane_recv.at[other]).wait()

    two_c = [gather(21, col_c, c, c, at_c)]
    half = pl.ds(32 * c, 32)
    near_c = pltpu.make_async_remote_copy(
        src_ref=near.at[:, half],
        dst_ref=near.at[:, half],
        send_sem=gather_send.at[14],
        recv_sem=gather_recv.at[14],
        device_id=at_c,
        device_id_type=MESH,
    )
    two_near = [
        pltpu.make_async_remote_copy(
            src_ref=two_own.at[half],
            dst_ref=near.at[(d + 2) % 4, half],
            send_sem=gather_send.at[22 + d],
            recv_sem=gather_recv.at[22 + d],
            device_id=beside(d),
            device_id_type=MESH,
        )
        for d in range(4)
    ]
    sum_one = [
        pltpu.make_async_remote_copy(
            src_ref=local.at[lax.rem(x + s, 4)],
            dst_ref=sum_x.at[x],
            send_sem=gather_send.at[25 + s],
            recv_sem=gather_recv.at[25 + s],
            device_id=at_x(s),
            device_id_type=MESH,
        )
        for s in (1, 2, 3)
    ]
    sum_two = ring(29, sum_y, y, 4, at_y)
    sum_three = ring(32, total, x, 4, at_x)

    def start(copies):
        for copy in copies:
            copy.start()

    def finish(copies):
        for copy in copies:
            copy.wait()

    start(three_x)

    def send_leaf(g, turn, n):
        place, d = LEAVES[n]
        return pltpu.make_async_remote_copy(
            src_ref=packed.at[block_of(place, turn), pl.ds(2 * g, 2)],
            dst_ref=raw.at[g, n],
            send_sem=raw_send,
            recv_sem=raw_recv.at[g],
            device_id=beside(turned(d, turn)),
            device_id_type=MESH,
        )

    @pl.loop(0, groups)
    def _(g):
        turn = turn_of(g)
        for n in range(len(LEAVES)):
            send_leaf(g, turn, n).start()

        @pl.when(g == 0)
        def _():
            @pl.loop(0, z)
            def _(other):
                greet(ready_z, (other * 2 + c, gy))

            @pl.when(c == 1)
            def _():
                greet(ready_c, at_c)

            @pl.loop(0, z)
            def _(other):
                two_z(other).start()

        @pl.when(g == 1)
        def _():
            finish(three_x)
            tile_y[y] = tile_x[0] + tile_x[1] + tile_x[2] + tile_x[3]
            start(three_y)

        @pl.when(g == 3)
        def _():
            @pl.when(z < 7)
            def _():
                pl.semaphore_wait(ready_z, 7 - z)

            @pl.loop(z + 1, 8)
            def _(other):
                two_z(other).start()

            finish(three_y)
            for k in range(4):
                tile_z[z, pl.ds(8 * k, 8), :] = tile_y[k]
            start(three_z)

        @pl.when(g == 4)
        def _():
            pl.loop(0, z)(from_plane)
            pl.loop(z + 1, 8)(from_plane)
            for k in range(8):
                col_c[c, pl.ds(8 * k, 8), :] = col_z[k]

            @pl.when(c == 0)
            def _():
                pl.semaphore_wait(ready_c, 1)

            start(two_c)

        @pl.when(g == 5)
        def _():
            finish(two_c)
            for k in range(8):
                for core in range(2):
                    flip[pl.ds(16 * k + 8 * core, 8), :] = col_c[core, pl.ds(8 * k, 8), :]
            two_own[...] = jnp.transpose(flip[...])[0:64, :]
            start(two_near)

        @pl.when(g < groups - 1)
        def _():
            load(g + 1).wait()
            pack(2 * g + 2)
            pack(2 * g + 3)

    finish(three_z)
    for k in range(8):
        tile_c[c, pl.ds(32 * k, 32), :] = tile_z[k]
    start(three_c)
    finish(three_c)
    for k in range(8):
        for core in range(2):
            high, low = split(tile_c[core, pl.ds(32 * k, 32), :])
            third[pl.ds(64 * k + 32 * core, 32), 0:128] = high
            third[pl.ds(64 * k + 32 * core, 32), 128:256] = low

    def times(value, weight, contract):
        dims = (((contract,), (0,)), ((), ()))
        out = sum(lax.dot_general(part, weight, dims, preferred_element_type=F32) for part in split(value))
        return out[:, 0:128] + out[:, 128:256]

    def contract_third(g):
        for i in range(0, ROWS, 2):
            rows = pl.ds(g * ROWS + i, 2)
            result = times(whole[rows].reshape(128, 512), third[...], 1).reshape(2, 64, 128)
            pair_three[rows] = result
            sums = jnp.sum(result * two_own[...][None], axis=1)
            local[g // 2, pl.ds(lax.rem(g, 2) * 8 + i, 2), :] = sums

    def send_part(g, turn, n):
        return pltpu.make_async_remote_copy(
            src_ref=sent.at[g, n],
            dst_ref=got.at[g, n],
            send_sem=part_send,
            recv_sem=part_recv.at[g, n],
            device_id=beside(turned(INNER[n][3], turn)),
            device_id_type=MESH,
        )

    def product(g, n):
        turn = turn_of(g)
        place, leaves, _, d = INNER[n]
        own = block_of(place, turn)
        pieces, weight = [[packed[own, 2 * g + h] for h in (0, 1)]], [weights[4]]
        for leaf in leaves:
            pieces.append([raw[g, leaf, h] for h in (0, 1)])
            weight.append(weights[turned((LEAVES[leaf][1] + 2) % 4, turn)])
        stacked = jnp.concatenate([jnp.concatenate(piece, axis=1) for piece in pieces], axis=0)
        result = times(stacked, jnp.concatenate(weight, axis=0), 0)
        if d is None:
            pair_two[pl.ds(g * ROWS, ROWS)] = result.reshape(ROWS, 32, 128)
        else:
            sent[g, n] = result

    def combine(g, n):
        _, _, parts, d = INNER[n]
        for part in parts:
            pltpu.make_async_copy(got.at[g, part], got.at[g, part], part_recv.at[g, part]).wait()
        more = sum(got[g, part] for part in parts) if parts else None
        if d is None:
            pair_two[pl.ds(g * ROWS, ROWS)] += more.reshape(ROWS, 32, 128)
        else:
            if parts:
                sent[g, n] += more
            send_part(g, turn_of(g), n).start()

    pl.loop(0, groups // 2)(contract_third)
    finish(two_near)
    near_c.start()
    pl.loop(groups // 2, groups)(contract_third)
    sum_x[x] = local[x]
    start(sum_one)
    near_c.wait()
    for k in range(5):
        high, low = split(two_own[...] if k == 4 else near[k])
        weights[k, :, 0:128] = high
        weights[k, :, 128:256] = low

    @pl.loop(0, groups + 3 * SKEW)
    def _(step):
        @pl.when(step < groups)
        def _():
            pltpu.make_async_copy(raw.at[step], raw.at[step], raw_recv.at[step]).wait()

        @pl.when(step < groups)
        def _():
            for n in STAGES[0]:
                product(step, n)
                combine(step, n)

        for late, nodes in enumerate(STAGES[1:], 1):
            g = step - late * SKEW

            @pl.when((g >= 0) & (g < groups))
            def _(g=g, nodes=nodes):
                for n in nodes:
                    combine(g, n)

        @pl.when(step < groups)
        def _():
            for n in range(2, 6):
                product(step, n)

        @pl.when(step == groups)
        def _():
            finish(sum_one)
            sum_y[y] = sum_x[0] + sum_x[1] + sum_x[2] + sum_x[3]
            start(sum_two)

        @pl.when(step == groups + 6)
        def _():
            finish(sum_two)
            total[x] = sum_y[0] + sum_y[1] + sum_y[2] + sum_y[3]
            start(sum_three)

    finish(sum_three)
    for k in range(4):
        mttkrp[pl.ds(16 * k, 16), :] = total[k]

    pltpu.make_async_copy(raw, raw, raw_send).wait()
    pltpu.make_async_copy(sent, sent, part_send).wait()


def keep(*refs):
    sources, targets, sem = refs[:3], refs[3:6], refs[6]
    copies = []
    for source, target, parts in zip(sources, targets, (8, 4, 1)):
        size = source.shape[0] // parts
        for n in range(parts):
            rows = pl.ds(n * size, size)
            copies.append(pltpu.make_async_copy(source.at[rows], target.at[rows], sem.at[len(copies)]))
    for copy in copies:
        copy.start()
    for copy in copies:
        copy.wait()


def per_device(tensor, two, three):
    rows = tensor.shape[0]
    groups, subs = rows // ROWS, rows // SUB
    shapes = ((rows, 64, 128), (rows, 32, 128), (rows, 128))
    hbm, vmem = pl.BlockSpec(memory_space=pl.ANY), pl.BlockSpec(memory_space=pltpu.VMEM)
    dma, regular = pltpu.SemaphoreType.DMA, pltpu.SemaphoreType.REGULAR
    results = pl.pallas_call(
        kernel,
        name="pair_operators",
        out_shape=tuple(pltpu.VMEM(shape, F32) for shape in shapes),
        in_specs=[hbm, pl.BlockSpec(memory_space=pltpu.HBM), pl.BlockSpec(memory_space=pltpu.HBM)],
        out_specs=(vmem, vmem, vmem),
        scratch_shapes=[
            pltpu.VMEM(tensor.shape, F32),
            pltpu.VMEM((8, 64), F32),
            pltpu.VMEM((2, 128), F32),
            pltpu.VMEM((16, subs, 64, 128), F32),
            pltpu.VMEM((groups, len(LEAVES), 2, 64, 128), F32),
            pltpu.VMEM((groups, 5, 256, 128), F32),
            pltpu.VMEM((groups, 5, 256, 128), F32),
            pltpu.VMEM((4, 8, 128), F32),
            pltpu.VMEM((4, 8, 128), F32),
            pltpu.VMEM((8, 32, 128), F32),
            pltpu.VMEM((2, 256, 128), F32),
            pltpu.VMEM((8, 8, 128), F32),
            pltpu.VMEM((2, 64, 128), F32),
            pltpu.VMEM((4, 64, 128), F32),
            pltpu.VMEM((64, 128), F32),
            pltpu.VMEM((5, 64, 256), BF16),
            pltpu.VMEM((512, 256), BF16),
            pltpu.VMEM((128, 128), F32),
            pltpu.VMEM((4, 16, 128), F32),
            pltpu.VMEM((4, 16, 128), F32),
            pltpu.VMEM((4, 16, 128), F32),
            pltpu.VMEM((4, 16, 128), F32),
            dma((groups,)),
            dma((2,)),
            dma,
            dma((groups,)),
            dma,
            dma((groups, 5)),
            dma((35,)),
            dma((35,)),
            regular,
            regular,
            dma((8,)),
            dma((8,)),
        ],
        cost_estimate=pl.CostEstimate(flops=7 << 30, bytes_accessed=22 << 20, transcendentals=0),
        compiler_params=pltpu.CompilerParams(collective_id=0, has_side_effects=True, vmem_limit_bytes=44 << 20),
    )(tensor, pltpu.with_memory_space_constraint(two.T, pltpu.HBM), pltpu.with_memory_space_constraint(three, pltpu.HBM))
    return pl.pallas_call(
        keep,
        name="keep",
        out_shape=tuple(jax.ShapeDtypeStruct(shape, F32) for shape in shapes),
        in_specs=[vmem] * 3,
        out_specs=(hbm, hbm, hbm),
        scratch_shapes=[dma((13,))],
        compiler_params=pltpu.CompilerParams(vmem_limit_bytes=4 << 20),
    )(*results)


def solution(mesh):
    return jax.shard_map(
        per_device,
        mesh=mesh,
        in_specs=(P("gx", "gy", None), P("gy", "gx"), P(("gx", "gy"), None)),
        out_specs=(P("gx", "gy", None), P("gx", "gy", None), P("gx", None)),
        check_vma=False,
    )
```
